32 devices in a mesh: groups: 2 (over y), ffn: 4 (over z), side: 2 (over x), head: 2 (over core).
Axes of the slice: x: 2, y: 2, z: 4, core: 2. Of those that a mesh axis runs over, the one named last changes fastest.
Arguments:
- resid: bfloat16 [64, 8192], P('groups', ('ffn', 'side')), parts along dimension 0, may hold values from -6 to 6
- queries: bfloat16 [80, 8192], P(('groups', 'ffn', 'side'), 'head'), parts along dimension 0, may hold values from -240 to 240
- cache_keys: bfloat16 [80, 128, 512], P(('groups', 'ffn', 'side'), None, 'head'), parts along dimension 0, may hold values from -6 to 6
- cache_values: bfloat16 [80, 128, 512], P(('groups', 'ffn', 'side'), None, 'head'), parts along dimension 0, may hold values from -6 to 6
- assign: int32 [64], P('groups'), parts along dimension 0, may hold values from 0 to 7, as said below
- lengths: int32 [64], P('groups'), parts along dimension 0, may hold values from 1 to 128, as said below
- out_weight: bfloat16 [8192, 8192], P('head', ('ffn', 'side')), may hold values from -0.0625 to 0.0625
- norm_gain: float32 [8192], replicated, may hold values from 0.1 to 1.9
- w_gate: bfloat16 [8192, 26624], P(None, ('ffn', 'side', 'head')), may hold values from -0.0625 to 0.0625
- w_up: bfloat16 [8192, 26624], P(None, ('ffn', 'side', 'head')), may hold values from -0.0625 to 0.0625
- w_down: bfloat16 [26624, 8192], P(('ffn', 'side', 'head')), may hold values from -0.0390625 to 0.0390625
Outputs:
- updated: bfloat16 [64, 8192], P(('groups', 'ffn', 'side', 'head')), parts along dimension 0
The draws below stay inside these ranges and needn't reach their ends.
There are 2 independent parts, one for each index of `groups`. The reference program is written for one: setup_inputs(seed, part) draws one part's arguments, and reference() takes and returns one part's arrays. A program takes and returns all parts, laid end to end along the dimension named above; an argument that names none is the same for every part. Nothing has to cross between parts.
Inputs may be any that keep to these rules, and one draw needn't show every extreme that they name: `assign`: each attention device receives at most 5 rows, and some device exactly 5. `lengths`: some row has exactly 128.
All inputs are finite; a program needn't handle non-finite values.
Results may differ from the reference program's by a relative error of at most 0.0054.
Values may be sent and summed in bfloat16 or wider, within the bound.
A program may use at most 192 MiB of HBM per device.

```python
import jax
import jax.numpy as jnp
from jax import lax

D = 8192
FF = 26624
HQ = 64
KVH = 4
HD = 128
CTX = 128
ATT = 8
CAP = 5
SLOTS = 40
ROWS = 32


def base_keys(key):
    return jnp.clip(jax.random.normal(key, (SLOTS, CTX, KVH * HD), jnp.float32), -6.0, 6.0)


def draw_cache_keys(key, part):
    shared = base_keys(key)
    return shared.astype(jnp.bfloat16)


def draw_queries(key, part):
    key = jax.random.fold_in(key, 12)
    first = jax.random.fold_in(key, 0)
    entries = jnp.clip(jax.random.normal(first, (SLOTS, HQ * HD), jnp.float32), -6.0, 6.0)
    return entries.astype(jnp.bfloat16)


def draw_lengths(key, part):
    key = jax.random.fold_in(key, 13)
    first, second = jax.random.split(key)
    drawn = jax.random.randint(first, (ROWS,), 1, CTX + 1, jnp.int32)
    longest = jax.random.randint(second, (), 0, ROWS, jnp.int32)
    return jnp.where(jnp.arange(ROWS, dtype=jnp.int32) == longest, CTX, drawn).astype(jnp.int32)


def draw_assign(key, part):
    key = jax.random.fold_in(key, 14)
    first, second, third = jax.random.split(key, 3)
    full_device = jax.random.randint(first, (), 0, ATT, jnp.int32)
    ids = jnp.arange(SLOTS, dtype=jnp.int32)
    scores = jax.random.randint(second, (SLOTS,), 0, 1 << 20, jnp.int32)
    scores = jnp.where(ids // CAP == full_device, -1, scores) * SLOTS + ids
    order = jnp.argsort(scores, stable=True).astype(jnp.int32)
    chosen = order[:ROWS]
    mixing = jax.random.permutation(third, ROWS)
    return (chosen[mixing] // CAP).astype(jnp.int32)


def block_scale(own_key, dims, cuts, least, high):
    gain, own = 1.0, jax.random.fold_in(own_key, 6)
    for axis_at, shards_of in cuts:
        heights = jnp.exp(jax.random.uniform(jax.random.fold_in(own, axis_at), (shards_of,), jnp.float32, least / len(cuts), high / len(cuts)))
        gain = gain * jnp.repeat(heights, dims[axis_at] // shards_of).reshape([-1 if axis == axis_at else 1 for axis in range(len(dims))])
    return gain


def scatter_about(rng, extent, deviation, bound, cuts=(), kind=jnp.bfloat16):
    result = deviation * jax.random.normal(rng, extent, jnp.float32)
    if cuts:
        result = result * block_scale(rng, extent, cuts, -0.22, 0.18)
    return jnp.clip(result, -bound, bound).astype(kind)


def setup_inputs(seed: int = 0, part: int = 0) -> dict:
    arg_keys = jax.random.split(jax.random.key(seed), 12)
    part_splits = jax.random.split(jax.random.fold_in(arg_keys[11], part), 12)
    return {
        "resid": scatter_about(part_splits[0], (ROWS, D), 1.0, 6.0, ((1, 8),)),
        "queries": draw_queries(jax.random.fold_in(jax.random.fold_in(arg_keys[11], part), 71), part),
        "cache_keys": draw_cache_keys(jax.random.fold_in(jax.random.fold_in(arg_keys[11], part), 71), part),
        "cache_values": scatter_about(part_splits[3], (SLOTS, CTX, KVH * HD), 1.0, 6.0, ((0, 8), (2, 2))),
        "assign": draw_assign(jax.random.fold_in(jax.random.fold_in(arg_keys[11], part), 71), part),
        "lengths": draw_lengths(jax.random.fold_in(jax.random.fold_in(arg_keys[11], part), 71), part),
        "out_weight": scatter_about(arg_keys[6], (HQ * HD, D), (HQ * HD) ** -0.5, 0.0625, ((0, 2), (1, 8))),
        "norm_gain": jnp.clip(1.0 + 0.18 * jax.random.normal(arg_keys[7], (D,), jnp.float32), 0.1, 1.9),
        "w_gate": scatter_about(arg_keys[8], (D, FF), D ** -0.5, 0.0625, ((1, 16),)),
        "w_up": scatter_about(arg_keys[9], (D, FF), D ** -0.5, 0.0625, ((1, 16),)),
        "w_down": scatter_about(arg_keys[10], (FF, D), FF ** -0.5, 0.0390625, ((0, 16),)),
    }


def slot_numbers(assign):
    owners = jnp.arange(ATT, dtype=jnp.int32)
    onehot = (assign[:, None] == owners[None, :]).astype(jnp.int32)
    before = jnp.cumsum(onehot, axis=0) - onehot
    rank = lax.optimization_barrier(jnp.sum(before * onehot, axis=1)).astype(jnp.int32)
    return (assign * CAP + rank).astype(jnp.int32)

def attend_row(items):
    query, keys, values, length = items
    group = HQ // KVH
    qh = query.reshape(KVH, group, HD).astype(jnp.float32)
    kh = keys.reshape(CTX, KVH, HD).astype(jnp.float32)
    vh = values.reshape(CTX, KVH, HD).astype(jnp.float32)
    scores = jnp.einsum('kgd,tkd->kgt', qh, kh) * (1.0 / math_sqrt(HD))
    mask = (jnp.arange(CTX, dtype=jnp.int32) < length)[None, None, :]
    top = lax.optimization_barrier(jnp.max(jnp.where(mask, scores, -1e+30), axis=-1, keepdims=True))
    weights = jnp.where(mask, jnp.exp(scores - top), 0.0)
    total = lax.optimization_barrier(jnp.sum(weights, axis=-1, keepdims=True))
    probs = (weights / total).astype(jnp.bfloat16)
    out = jnp.einsum('kgt,tkd->kgd', probs.astype(jnp.float32), vh)
    return out.reshape(HQ * HD).astype(jnp.bfloat16)

def math_sqrt(value):
    return float(value) ** 0.5

def reference(resid, queries, cache_keys, cache_values, assign, lengths, out_weight, norm_gain, w_gate, w_up, w_down):
    slot_of = slot_numbers(assign)
    attended = lax.map(attend_row, (queries[slot_of], cache_keys[slot_of], cache_values[slot_of], lengths))
    mixed = resid.astype(jnp.float32) + jnp.dot(attended, out_weight, preferred_element_type=jnp.float32)
    meansq = lax.optimization_barrier(jnp.mean(mixed * mixed, axis=1, keepdims=True))
    normed = (mixed * lax.rsqrt(meansq + 1e-05) * norm_gain[None, :]).astype(jnp.bfloat16)
    gate = jnp.dot(normed, w_gate, preferred_element_type=jnp.float32)
    up = jnp.dot(normed, w_up, preferred_element_type=jnp.float32)
    hidden = (jax.nn.silu(gate) * up).astype(jnp.bfloat16)
    summed = mixed + jnp.dot(hidden, w_down, preferred_element_type=jnp.float32)
    return summed.astype(jnp.bfloat16)
```

```python
import functools

import jax
import jax.numpy as jnp
from jax import lax
from jax.experimental import pallas as pl
from jax.experimental.pallas import tpu as pltpu
from jax.sharding import PartitionSpec as P

D = 8192
HD = 128


def slot_numbers(assign, att_count, cap):
    owners = jnp.arange(att_count, dtype=jnp.int32)
    onehot = (assign[:, None] == owners[None, :]).astype(jnp.int32)
    before = jnp.cumsum(onehot, axis=0) - onehot
    rank = jnp.sum(before * onehot, axis=1)
    return assign * cap + rank


def shards(
    resid,
    queries,
    cache_keys,
    cache_values,
    assign,
    lengths,
    out_weight,
    norm_gain,
    w_gate,
    w_up,
    w_down,
):
    cap = queries.shape[0]
    ctx = cache_keys.shape[1]
    kv_local = cache_keys.shape[2] // HD
    q_local = queries.shape[1] // HD
    group = q_local // kv_local
    cols = resid.shape[1]
    att_count = lax.axis_size(("ffn", "side"))
    device = lax.axis_index(("ffn", "side"))
    slot_of = slot_numbers(assign, att_count, cap)
    wanted = device * cap + jnp.arange(cap, dtype=jnp.int32)
    match = slot_of[:, None] == wanted[None, :]
    slot_len = jnp.sum(jnp.where(match, lengths[:, None], 0), axis=0)
    qh = queries.reshape(cap, kv_local, group, HD)
    kh = cache_keys.reshape(cap, ctx, kv_local, HD)
    vh = cache_values.reshape(cap, ctx, kv_local, HD)
    scores = jnp.einsum("ckgd,ctkd->ckgt", qh, kh, preferred_element_type=jnp.float32) * (
        1.0 / float(HD) ** 0.5
    )
    mask = (jnp.arange(ctx, dtype=jnp.int32)[None, :] < slot_len[:, None])[:, None, None, :]
    top = jnp.max(jnp.where(mask, scores, -1e30), axis=-1, keepdims=True)
    weights = jnp.where(mask, jnp.exp(scores - top), 0.0)
    total = jnp.sum(weights, axis=-1, keepdims=True)
    total = jnp.where(slot_len[:, None, None, None] > 0, total, 1.0)
    probs = (weights / total).astype(jnp.bfloat16)
    attended = jnp.einsum("ckgt,ctkd->ckgd", probs, vh, preferred_element_type=jnp.float32)
    attended = attended.astype(jnp.bfloat16).reshape(cap, q_local * HD)
    partial_out = jnp.dot(
        lax.all_gather(attended, ("ffn", "side"), axis=0, tiled=True),
        out_weight,
        preferred_element_type=jnp.float32,
    )
    slot_out = lax.psum(partial_out, "head")
    mixed = resid.astype(jnp.float32) + jnp.take(slot_out, slot_of, axis=0)
    col_start = device * cols
    squares = jnp.sum(mixed * mixed, axis=1)
    meansq = lax.psum(squares, ("ffn", "side")) / D
    gain_local = lax.dynamic_slice_in_dim(norm_gain, col_start, cols, 0)
    normed = (mixed * lax.rsqrt(meansq + 1e-05)[:, None] * gain_local[None, :]).astype(jnp.bfloat16)
    piece = lax.all_gather(normed, ("ffn", "side"), axis=1, tiled=True)
    gate = jnp.dot(piece, w_gate, preferred_element_type=jnp.float32)
    up = jnp.dot(piece, w_up, preferred_element_type=jnp.float32)
    hidden = (jax.nn.silu(gate) * up).astype(jnp.bfloat16)
    product = jnp.dot(hidden, w_down, preferred_element_type=jnp.float32)
    carried = mixed * 0.5
    block = lax.dynamic_slice_in_dim(product, col_start, cols, 1) + carried
    summed = lax.psum_scatter(
        lax.dynamic_update_slice_in_dim(product, block, col_start, 1),
        ("ffn", "side", "head"),
        scatter_dimension=0,
        tiled=True,
    )
    return summed.astype(jnp.bfloat16)


NZ, NX, NH = 4, 2, 2
GU_PAIRS = 11
WD_SLOTS = 6
EARLY = 3
F32 = jnp.float32
BF16 = jnp.bfloat16


def iota(shape, dim):
    return lax.broadcasted_iota(jnp.int32, shape, dim)


def fused_kernel(
    assign_ref, lengths_ref, gain_ref, resid_ref, q_ref, k_ref, v_ref,
    wo_hbm, wg_hbm, wu_hbm, wd_hbm,
    out_ref,
    wo, gu, wd, qf, place, att, lhs, expart, exrecv, mixed, nrm, sq, acc, hidden,
    prod, hrecv, s1, xsend, xrecv, s2, zf, zsend, zrecv, facc,
    wo_sem, gu_sem, wd_sem, att_send, att_recv, ex_send, ex_recv, nrm_send, nrm_recv,
    sq_send, sq_recv, h_send, h_recv, x_send, x_recv, z_send, z_recv,
):
    z, x, h = lax.axis_index("ffn"), lax.axis_index("side"), lax.axis_index("head")
    dev = z * NX + x
    own = dev * NH + h
    other_x, other_h = 1 - x, 1 - h
    rows, width = lhs.shape
    half = nrm.shape[2]
    slabs = nrm.shape[0]
    cap = q_ref.shape[0]
    group = qf.shape[0] // cap
    kv = k_ref.shape[2] // HD

    def z_at(step):
        return lax.rem(z + step, NZ)

    def to_z(step):
        return {"ffn": z_at(step)}

    to_x, to_h = {"side": other_x}, {"head": other_h}

    def remote(src, dst, send, recv, where):
        return pltpu.make_async_remote_copy(
            src_ref=src, dst_ref=dst, send_sem=send, recv_sem=recv,
            device_id=where, device_id_type=pl.DeviceIdType.MESH,
        )

    def slab_at(i):
        zi = z_at(i)
        xi = lax.rem(x + lax.div(i, NZ), NX)
        hi = lax.rem(h + lax.div(i, NZ * NX), NH)
        return (zi * NX + xi) * NH + hi

    def wo_copy(j):
        start = other_h if j == 0 else h
        return pltpu.make_async_copy(
            wo_hbm.at[:, pl.ds(pl.multiple_of(start * half, half), half)], wo.at[j], wo_sem.at[j]
        )

    def gu_copy(i, j):
        slot = lax.rem(i, GU_PAIRS) * 2 + j
        src = (wg_hbm, wu_hbm)[j]
        start = pl.multiple_of(slab_at(i) * half, half)
        return pltpu.make_async_copy(src.at[pl.ds(start, half), :], gu.at[slot], gu_sem.at[slot])

    def wd_copy(c):
        slot = lax.rem(c, WD_SLOTS)
        start = pl.multiple_of(c * half, half)
        return pltpu.make_async_copy(wd_hbm.at[:, pl.ds(start, half)], wd.at[slot], wd_sem.at[slot])

    def start_pair(i, carry=0):
        gu_copy(i, 0).start()
        gu_copy(i, 1).start()
        return carry

    wo_copy(0).start()
    wo_copy(1).start()
    lax.fori_loop(0, EARLY, start_pair, 0)

    barrier = pltpu.get_barrier_semaphore()
    for where in (to_z(1), to_z(2), to_z(3), to_x, to_h):
        pl.semaphore_signal(barrier, inc=1, device_id=where, device_id_type=pl.DeviceIdType.MESH)

    a_row = jnp.broadcast_to(assign_ref[...].astype(F32), (rows, rows))
    len_row = lengths_ref[...].astype(F32)
    down, across = iota((rows, rows), 0), iota((rows, rows), 1)
    a_col = jnp.sum(jnp.where(down == across, a_row, 0.0), axis=1, keepdims=True)
    rank_row = jnp.sum(
        jnp.where((a_col == a_row) & (down < across), 1.0, 0.0), axis=0, keepdims=True
    )
    slot_row = assign_ref[...].astype(F32) * cap + rank_row
    cr = iota((group * cap, 1), 0)
    of_slot = cr - cap * ((cr * 205) >> 10)
    wanted = (dev * cap + of_slot).astype(F32)
    slot_len = jnp.sum(
        jnp.where(jnp.broadcast_to(slot_row, (group * cap, rows)) == wanted, len_row, 0.0),
        axis=1, keepdims=True,
    )
    ctx = k_ref.shape[1]
    mask = iota((group * cap, ctx), 1).astype(F32) < slot_len
    for k in range(kv):
        for g in range(group):
            at = (k * group + g) * HD
            qf[g * cap:(g + 1) * cap, :] = q_ref[:, at:at + HD].astype(F32)
        qk = qf[...].astype(BF16)
        keys = k_ref[:, :, k * HD:(k + 1) * HD].reshape(cap * ctx, HD)
        values = v_ref[:, :, k * HD:(k + 1) * HD].reshape(cap * ctx, HD)
        wide = lax.dot_general(qk, keys, (((1,), (1,)), ((), ())), preferred_element_type=F32)
        scores = jnp.zeros((group * cap, ctx), F32)
        for c in range(cap):
            scores = jnp.where(of_slot == c, wide[:, c * ctx:(c + 1) * ctx], scores)
        scores = scores * (1.0 / float(HD) ** 0.5)
        top = jnp.max(jnp.where(mask, scores, -1e30), axis=-1, keepdims=True)
        weights = jnp.where(mask, jnp.exp(scores - top), 0.0)
        total = jnp.sum(weights, axis=-1, keepdims=True)
        total = jnp.where(slot_len > 0.0, total, 1.0)
        probs = weights / total
        spread = jnp.concatenate(
            [jnp.where(of_slot == c, probs, 0.0) for c in range(cap)], axis=1
        ).astype(BF16)
        att[dev, k] = jnp.dot(spread, values, preferred_element_type=F32).astype(BF16)

    pl.semaphore_wait(barrier, 5)

    def att_copy(d, sem, where):
        return remote(att.at[d], att.at[d], att_send.at[sem], att_recv.at[d], where)

    att_out = [att_copy(dev, t - 1, to_z(t)) for t in range(1, NZ)]
    att_out.append(att_copy(dev, NZ - 1, to_x))
    for copy in att_out:
        copy.start()

    lax.fori_loop(EARLY, GU_PAIRS, start_pair, 0)

    def start_wd(c, carry):
        wd_copy(c).start()
        return carry

    lax.fori_loop(0, WD_SLOTS, start_wd, 0)

    pos = iota((rows, 1), 0)
    each = rows // (NZ * NX * NH)
    row_of = ((pos // each) % NZ) * (NX * NH * each) + ((pos // (each * NZ)) % NX) * (NH * each)
    row_of = row_of + (pos // (each * NZ * NX)) * each + pos % each
    row_pick = across == row_of
    a_pos = jnp.sum(jnp.where(row_pick, a_row, 0.0), axis=1, keepdims=True)
    rank_pos = jnp.sum(
        jnp.where(row_pick, jnp.broadcast_to(rank_row, (rows, rows)), 0.0), axis=1, keepdims=True
    )
    target = a_pos * (group * cap) + rank_pos
    lane = iota((rows, NZ * NX * group * cap), 1).astype(F32)
    for g in range(group):
        place[g * rows:(g + 1) * rows, :] = jnp.where(lane == target + g * cap, 1.0, 0.0).astype(BF16)
    resid_half = resid_ref[:, pl.ds(pl.multiple_of(h * half, half), half)]
    mixed[...] = jnp.dot(row_pick.astype(F32).astype(BF16), resid_half, preferred_element_type=F32)

    for t in range(1, NZ):
        d = z_at(t) * NX + x
        att_copy(d, 0, to_x).wait_recv()
        fwd = att_copy(d, NZ - 1 + t, to_x)
        fwd.start()
        att_out.append(fwd)
    for t in range(NZ):
        d = z_at(t) * NX + other_x
        att_copy(d, 0, to_x).wait_recv()
    for k in range(kv):
        blocks = att[:, k].reshape(NZ * NX * group * cap, HD)
        moved = jnp.dot(place[...], blocks, preferred_element_type=F32).astype(BF16)
        for g in range(group):
            at = (k * group + g) * HD
            lhs[:, at:at + HD] = moved[g * rows:(g + 1) * rows, :]
    for copy in att_out:
        copy.wait_send()

    depth = 512

    def project(j):
        def part(i, total):
            start = pl.multiple_of(i * depth, depth)
            return total + jnp.dot(
                lhs[:, pl.ds(start, depth)], wo[j, pl.ds(start, depth), :],
                preferred_element_type=F32,
            )

        return lax.fori_loop(0, width // depth, part, jnp.zeros((rows, half), F32))

    wo_copy(0).wait()
    expart[...] = project(0)
    exchange = remote(expart, exrecv, ex_send, ex_recv, to_h)
    exchange.start()
    wo_copy(1).wait()
    mixed[...] = mixed[...] + project(1)
    exchange.wait()
    mix = mixed[...] + exrecv[...]
    mixed[...] = mix
    gains = gain_ref[0:1, pl.ds(pl.multiple_of(own * half, half), half)]
    nrm[own] = (mix * gains).astype(BF16)

    def nrm_copy(s, sem, where):
        return remote(nrm.at[s], nrm.at[s], nrm_send.at[sem], nrm_recv.at[s], where)

    for t in range(1, NZ):
        nrm_copy(own, t - 1, to_z(t)).start()
    nrm_copy(own, NZ - 1, to_x).start()
    nrm_copy(own, NZ, to_h).start()

    squares = jnp.sum(mix * mix, axis=1, keepdims=True)
    eye = iota((rows, HD), 0) == iota((rows, HD), 1)
    squares_row = jnp.sum(jnp.where(eye, squares, 0.0), axis=0, keepdims=True)
    sq[0] = jnp.broadcast_to(squares_row, (8, HD))

    def sq_copy(t):
        src, where = (0, to_z(t)) if t < NZ else ((NZ, to_x) if t == NZ else (NZ + 2, to_h))
        dst = t if t < NZ else (NZ + 1 if t == NZ else NZ + 3)
        return remote(sq.at[src], sq.at[dst], sq_send.at[t - 1], sq_recv.at[t - 1], where)

    for t in range(1, NZ):
        sq_copy(t).start()

    acc[...] = jnp.zeros_like(acc)

    def gate_up(i, carry):
        s = slab_at(i)

        @pl.when(i > 0)
        def _():
            nrm_copy(s, 0, to_h).wait_recv()

        @pl.when((i > 0) & (i < NZ))
        def _():
            nrm_copy(s, NZ + i, to_x).start()

        @pl.when((i > 0) & (i < NZ * NX))
        def _():
            nrm_copy(s, 2 * NZ - 1 + i, to_h).start()

        @pl.when(i == NZ * NX)
        def _():
            for t in range(1, NZ):
                sq_copy(t).wait()
            sq[NZ] = sq[0] + sq[1] + sq[2] + sq[3]
            sq_copy(NZ).start()

        @pl.when(i == NZ * NX + NZ)
        def _():
            sq_copy(NZ).wait()
            sq[NZ + 2] = sq[NZ] + sq[NZ + 1]
            sq_copy(NZ + 1).start()

        slot = lax.rem(i, GU_PAIRS) * 2
        block = nrm[s]
        gu_copy(i, 0).wait()
        acc[0] += jnp.dot(block, gu[slot], preferred_element_type=F32)
        gu_copy(i, 1).wait()
        acc[1] += jnp.dot(block, gu[slot + 1], preferred_element_type=F32)

        @pl.when(i + GU_PAIRS < slabs)
        def _():
            start_pair(i + GU_PAIRS)

        return carry

    lax.fori_loop(0, slabs, gate_up, 0)
    sq_copy(NZ + 1).wait()
    total_row = jnp.broadcast_to((sq[NZ + 2] + sq[NZ + 3])[0:1], (rows, HD))
    total = jnp.sum(jnp.where(eye, total_row, 0.0), axis=1, keepdims=True)
    scale = lax.rsqrt(total / D + 1e-05)
    gate = acc[0] * scale
    up = acc[1] * scale
    hidden[...] = (gate / (1.0 + jnp.exp(-gate)) * up).astype(BF16)

    batches = prod.shape[0]
    per = slabs // batches
    span = prod.shape[2]
    seg = zf.shape[3]
    hrows = rows // NH
    xrows = hrows // NX

    def multiply(b):
        def chunk(j, carry):
            c = b * per + j
            wd_copy(c).wait()
            term = jnp.dot(hidden[...], wd[lax.rem(c, WD_SLOTS)], preferred_element_type=F32)
            term = term + jnp.where(c == own, 1.0, 0.0) * mixed[...]
            prod[b, :, pl.ds(pl.multiple_of(j * half, half), half)] = term

            @pl.when(c + WD_SLOTS < slabs)
            def _():
                wd_copy(c + WD_SLOTS).start()

            return carry

        lax.fori_loop(0, per, chunk, 0)

    def h_copy(b):
        src = prod.at[b, pl.ds(pl.multiple_of(other_h * hrows, hrows), hrows), :]
        return remote(src, hrecv.at[b], h_send.at[b], h_recv.at[b], to_h)

    def x_copy(b):
        return remote(xsend.at[b], xrecv.at[b], x_send.at[b], x_recv.at[b], to_x)

    def z_copy(b, t):
        sem = b * (NZ - 1) + t - 1
        return remote(zsend.at[b, z_at(t)], zrecv.at[b, t - 1], z_send.at[sem], z_recv.at[sem], to_z(t))

    def stage_x(b):
        h_copy(b).wait()
        s1[b] = prod[b, pl.ds(pl.multiple_of(h * hrows, hrows), hrows), :] + hrecv[b]
        there = s1[b, pl.ds(pl.multiple_of(other_x * xrows, xrows), xrows), :]
        xsend[b] = jnp.concatenate([there[:, :span // 2], there[:, span // 2:]], axis=0).astype(BF16)
        x_copy(b).start()

    def stage_z(b):
        x_copy(b).wait()
        here = s1[b, pl.ds(pl.multiple_of(x * xrows, xrows), xrows), :]
        came = xrecv[b].astype(F32)
        s2[b] = here + jnp.concatenate([came[:xrows], came[xrows:]], axis=1)
        for q in range(NZ):
            for m in range(span // seg):
                zf[b, q, m * each:(m + 1) * each, :] = s2[b, q * each:(q + 1) * each, m * seg:(m + 1) * seg]
        zsend[b] = zf[b].astype(BF16)
        for t in range(1, NZ):
            z_copy(b, t).start()

    def stage_out(b):
        for t in range(1, NZ):
            z_copy(b, t).wait()
        total = zf[b, z]
        for t in range(1, NZ):
            total = total + zrecv[b, t - 1].astype(F32)
        facc[b] = total
        for m in range(span // seg):
            at = b * span + m * seg
            out_ref[:, at:at + seg] = facc[b, m * each:(m + 1) * each, :].astype(BF16)

    for step in range(batches + 3):
        if step < batches:
            multiply(step)
            h_copy(step).start()
        if 0 <= step - 1 < batches:
            stage_x(step - 1)
        if 0 <= step - 2 < batches:
            stage_z(step - 2)
        if 0 <= step - 3 < batches:
            stage_out(step - 3)

    for t in range(1, NZ):
        nrm_copy(own, t - 1, to_z(t)).wait_send()
    nrm_copy(own, NZ - 1, to_x).wait_send()
    nrm_copy(own, NZ, to_h).wait_send()
    for i in range(1, NZ):
        nrm_copy(own, NZ + i, to_x).wait_send()
    for i in range(1, NZ * NX):
        nrm_copy(own, 2 * NZ - 1 + i, to_h).wait_send()


def fused(
    resid, queries, cache_keys, cache_values, assign, lengths,
    out_weight, norm_gain, w_gate, w_up, w_down,
):
    rows, cols = resid.shape
    cap = queries.shape[0]
    ff = w_gate.shape[1]
    half = cols // NH
    slabs = NZ * NX * NH
    kv = cache_keys.shape[2] // HD
    group = queries.shape[1] // HD // kv
    batches = 4
    span = slabs * half // batches
    each = rows // slabs
    seg = span * each // 16
    vmem = pl.BlockSpec(memory_space=pltpu.VMEM)
    hbm = pl.BlockSpec(memory_space=pl.ANY)
    dma = pltpu.SemaphoreType.DMA
    V = pltpu.VMEM
    weights = (out_weight.size + 3 * w_gate.size)
    return pl.pallas_call(
        fused_kernel,
        out_shape=jax.ShapeDtypeStruct((each, slabs * half), BF16),
        in_specs=[vmem] * 7 + [hbm] * 4,
        out_specs=vmem,
        scratch_shapes=[
            V((NH, out_weight.shape[0], half), BF16),
            V((2 * GU_PAIRS, half, ff), BF16),
            V((WD_SLOTS, ff, half), BF16),
            V((group * cap, HD), F32),
            V((group * rows, NZ * NX * group * cap), BF16),
            V((NZ * NX, kv, group * cap, HD), BF16),
            V((rows, out_weight.shape[0]), BF16),
            V((rows, half), F32),
            V((rows, half), F32),
            V((rows, half), F32),
            V((slabs, rows, half), BF16),
            V((NZ + 4, 8, HD), F32),
            V((2, rows, ff), F32),
            V((rows, ff), BF16),
            V((batches, rows, span), F32),
            V((batches, rows // NH, span), F32),
            V((batches, rows // NH, span), F32),
            V((batches, 16, span // 2), BF16),
            V((batches, 16, span // 2), BF16),
            V((batches, 8, span), F32),
            V((batches, NZ, 16, seg), F32),
            V((batches, NZ, 16, seg), BF16),
            V((batches, NZ - 1, 16, seg), BF16),
            V((batches, 16, seg), F32),
            dma((NH,)),
            dma((2 * GU_PAIRS,)),
            dma((WD_SLOTS,)),
            dma((2 * NZ,)),
            dma((NZ * NX,)),
            dma(()),
            dma(()),
            dma((2 * NZ + NZ * NX,)),
            dma((slabs,)),
            dma((NZ + 1,)),
            dma((NZ + 1,)),
            dma((batches,)),
            dma((batches,)),
            dma((batches,)),
            dma((batches,)),
            dma((batches * (NZ - 1),)),
            dma((batches * (NZ - 1),)),
        ],
        cost_estimate=pl.CostEstimate(
            flops=2 * rows * weights, bytes_accessed=2 * weights, transcendentals=rows * ff
        ),
        compiler_params=pltpu.CompilerParams(
            collective_id=0, has_side_effects=True, vmem_limit_bytes=63 * 1024 * 1024
        ),
    )(
        assign.reshape(1, rows), lengths.reshape(1, rows), norm_gain.reshape(1, -1),
        resid, queries, cache_keys, cache_values, out_weight, w_gate, w_up, w_down,
    )


def solution(mesh):
    in_specs = (
        P("groups", ("ffn", "side")),
        P(("groups", "ffn", "side"), "head"),
        P(("groups", "ffn", "side"), None, "head"),
        P(("groups", "ffn", "side"), None, "head"),
        P("groups"),
        P("groups"),
        P("head", ("ffn", "side")),
        P(),
        P(None, ("ffn", "side", "head")),
        P(None, ("ffn", "side", "head")),
        P(("ffn", "side", "head"), None),
    )
    out_specs = P(("groups", "ffn", "side", "head"), None)
    sizes = (mesh.shape["ffn"], mesh.shape["side"], mesh.shape["head"])
    body = fused if sizes == (NZ, NX, NH) else shards
    return jax.shard_map(body, mesh=mesh, in_specs=in_specs, out_specs=out_specs, check_vma=False)
```

```python
import functools

import jax
import jax.numpy as jnp
from jax import lax
from jax.experimental import pallas as pl
from jax.experimental.pallas import tpu as pltpu
from jax.sharding import PartitionSpec as P

D = 8192
HD = 128


def slot_numbers(assign, att_count, cap):
    owners = jnp.arange(att_count, dtype=jnp.int32)
    onehot = (assign[:, None] == owners[None, :]).astype(jnp.int32)
    before = jnp.cumsum(onehot, axis=0) - onehot
    rank = jnp.sum(before * onehot, axis=1)
    return assign * cap + rank


def shards(
    resid,
    queries,
    cache_keys,
    cache_values,
    assign,
    lengths,
    out_weight,
    norm_gain,
    w_gate,
    w_up,
    w_down,
):
    cap = queries.shape[0]
    ctx = cache_keys.shape[1]
    kv_local = cache_keys.shape[2] // HD
    q_local = queries.shape[1] // HD
    group = q_local // kv_local
    cols = resid.shape[1]
    att_count = lax.axis_size(("ffn", "side"))
    device = lax.axis_index(("ffn", "side"))
    slot_of = slot_numbers(assign, att_count, cap)
    wanted = device * cap + jnp.arange(cap, dtype=jnp.int32)
    match = slot_of[:, None] == wanted[None, :]
    slot_len = jnp.sum(jnp.where(match, lengths[:, None], 0), axis=0)
    qh = queries.reshape(cap, kv_local, group, HD)
    kh = cache_keys.reshape(cap, ctx, kv_local, HD)
    vh = cache_values.reshape(cap, ctx, kv_local, HD)
    scores = jnp.einsum("ckgd,ctkd->ckgt", qh, kh, preferred_element_type=jnp.float32) * (
        1.0 / float(HD) ** 0.5
    )
    mask = (jnp.arange(ctx, dtype=jnp.int32)[None, :] < slot_len[:, None])[:, None, None, :]
    top = jnp.max(jnp.where(mask, scores, -1e30), axis=-1, keepdims=True)
    weights = jnp.where(mask, jnp.exp(scores - top), 0.0)
    total = jnp.sum(weights, axis=-1, keepdims=True)
    total = jnp.where(slot_len[:, None, None, None] > 0, total, 1.0)
    probs = (weights / total).astype(jnp.bfloat16)
    attended = jnp.einsum("ckgt,ctkd->ckgd", probs, vh, preferred_element_type=jnp.float32)
    attended = attended.astype(jnp.bfloat16).reshape(cap, q_local * HD)
    partial_out = jnp.dot(
        lax.all_gather(attended, ("ffn", "side"), axis=0, tiled=True),
        out_weight,
        preferred_element_type=jnp.float32,
    )
    slot_out = lax.psum(partial_out, "head")
    mixed = resid.astype(jnp.float32) + jnp.take(slot_out, slot_of, axis=0)
    col_start = device * cols
    squares = jnp.sum(mixed * mixed, axis=1)
    meansq = lax.psum(squares, ("ffn", "side")) / D
    gain_local = lax.dynamic_slice_in_dim(norm_gain, col_start, cols, 0)
    normed = (mixed * lax.rsqrt(meansq + 1e-05)[:, None] * gain_local[None, :]).astype(jnp.bfloat16)
    piece = lax.all_gather(normed, ("ffn", "side"), axis=1, tiled=True)
    gate = jnp.dot(piece, w_gate, preferred_element_type=jnp.float32)
    up = jnp.dot(piece, w_up, preferred_element_type=jnp.float32)
    hidden = (jax.nn.silu(gate) * up).astype(jnp.bfloat16)
    product = jnp.dot(hidden, w_down, preferred_element_type=jnp.float32)
    carried = mixed * 0.5
    block = lax.dynamic_slice_in_dim(product, col_start, cols, 1) + carried
    summed = lax.psum_scatter(
        lax.dynamic_update_slice_in_dim(product, block, col_start, 1),
        ("ffn", "side", "head"),
        scatter_dimension=0,
        tiled=True,
    )
    return summed.astype(jnp.bfloat16)


NZ, NX, NH = 4, 2, 2
PAIRS = 11
WD_SLOTS = 3
WO_PAIRS = 4
EARLY = 2
RUNS = ((0,), (1, 2), (3, 4, 5), (6,), (7, 8, 9, 10), (11, 12, 13), (14, 15))
STEPS = (
    (0, 0, 0), (0, 0, 1), (0, 1, 0), (1, 0, 0), (2, 0, 0), (3, 0, 0), (0, 1, 1), (1, 1, 0),
    (2, 1, 0), (3, 1, 0), (1, 0, 1), (2, 0, 1), (3, 0, 1), (1, 1, 1), (2, 1, 1), (3, 1, 1),
)
F32 = jnp.float32
BF16 = jnp.bfloat16


def iota(shape, dim):
    return lax.broadcasted_iota(jnp.int32, shape, dim)


def fused_kernel(
    assign_ref, lengths_ref, gain_ref, resid_ref, q_ref, k_ref, v_ref,
    wo_hbm, wg_hbm, wu_hbm, wd_hbm,
    out_ref,
    gu, wd, qf, place, att, lhs, expart, exrecv, mixed, nrm, sq, acc, hidden,
    prod, hrecv, s1, zf, zsend, zrecv, facc,
    wo_sem, gu_sem, wd_sem, att_send, att_recv, ex_send, ex_recv, nrm_send, nrm_recv,
    sq_send, sq_recv, h_send, h_recv, z_send, z_recv,
):
    z, x, h = lax.axis_index("ffn"), lax.axis_index("side"), lax.axis_index("head")
    dev = z * NX + x
    own = dev * NH + h
    other_x, other_h = 1 - x, 1 - h
    rows, width = lhs.shape
    half = nrm.shape[2]
    slabs = nrm.shape[0]
    cap = q_ref.shape[0]
    group = qf.shape[0] // cap
    kv = k_ref.shape[2] // HD

    def z_at(step):
        high = lax.rem(lax.div(z, 2) + step // 2, 2)
        return high * 2 + lax.rem(z + step, 2)

    def to_z(step):
        return {"ffn": z_at(step)}

    to_x, to_h = {"side": other_x}, {"head": other_h}

    def remote(src, dst, send, recv, where):
        return pltpu.make_async_remote_copy(
            src_ref=src, dst_ref=dst, send_sem=send, recv_sem=recv,
            device_id=where, device_id_type=pl.DeviceIdType.MESH,
        )

    def chip(p):
        return z_at(p // 2), lax.rem(x + p, NX)

    def slab_at(i):
        dz, dx, dh = STEPS[i]
        return (z_at(dz) * NX + lax.rem(x + dx, NX)) * NH + lax.rem(h + dh, NH)

    def wo_copy(m):
        src = wo_hbm.at[pl.ds(m * half, half), :]
        dst = gu.at[m // WO_PAIRS, m % WO_PAIRS, :, pl.ds(0, wo_hbm.shape[1])]
        return pltpu.make_async_copy(src, dst, wo_sem.at[m])

    def gu_copy(i, j):
        slot = (i + WO_PAIRS) % PAIRS
        src = (wg_hbm, wu_hbm)[j]
        start = pl.multiple_of(slab_at(i) * half, half)
        return pltpu.make_async_copy(src.at[pl.ds(start, half), :], gu.at[j, slot], gu_sem.at[j, slot])

    def wd_copy(b):
        slot = b % WD_SLOTS
        span = wd.shape[2]
        return pltpu.make_async_copy(wd_hbm.at[:, pl.ds(b * span, span)], wd.at[slot], wd_sem.at[slot])

    def start_pair(i):
        gu_copy(i, 0).start()
        gu_copy(i, 1).start()

    barrier = pltpu.get_barrier_semaphore()
    for p in range(1, NZ * NX):
        zi, xi = chip(p)
        where = {"ffn": zi, "side": xi}
        pl.semaphore_signal(barrier, inc=1, device_id=where, device_id_type=pl.DeviceIdType.MESH)
    pl.semaphore_signal(barrier, inc=1, device_id=to_h, device_id_type=pl.DeviceIdType.MESH)
    for m in range(2 * WO_PAIRS):
        wo_copy(m).start()
    for i in range(EARLY):
        start_pair(i)

    a_row = jnp.broadcast_to(assign_ref[...].astype(F32), (rows, rows))
    len_row = lengths_ref[...].astype(F32)
    down, across = iota((rows, rows), 0), iota((rows, rows), 1)
    a_col = jnp.sum(jnp.where(down == across, a_row, 0.0), axis=1, keepdims=True)
    rank_row = jnp.sum(
        jnp.where((a_col == a_row) & (down < across), 1.0, 0.0), axis=0, keepdims=True
    )
    slot_row = assign_ref[...].astype(F32) * cap + rank_row
    cr = iota((group * cap, 1), 0)
    of_slot = cr - cap * ((cr * 205) >> 10)
    wanted = (dev * cap + of_slot).astype(F32)
    slot_len = jnp.sum(
        jnp.where(jnp.broadcast_to(slot_row, (group * cap, rows)) == wanted, len_row, 0.0),
        axis=1, keepdims=True,
    )
    ctx = k_ref.shape[1]
    mask = iota((group * cap, ctx), 1).astype(F32) < slot_len
    for k in range(kv):
        for g in range(group):
            at = (k * group + g) * HD
            qf[g * cap:(g + 1) * cap, :] = q_ref[:, at:at + HD].astype(F32)
        qk = qf[...].astype(BF16)
        keys = k_ref[:, :, k * HD:(k + 1) * HD].reshape(cap * ctx, HD)
        values = v_ref[:, :, k * HD:(k + 1) * HD].reshape(cap * ctx, HD)
        wide = lax.dot_general(qk, keys, (((1,), (1,)), ((), ())), preferred_element_type=F32)
        scores = jnp.zeros((group * cap, ctx), F32)
        for c in range(cap):
            scores = jnp.where(of_slot == c, wide[:, c * ctx:(c + 1) * ctx], scores)
        scores = scores * (1.0 / float(HD) ** 0.5)
        top = jnp.max(jnp.where(mask, scores, -1e30), axis=-1, keepdims=True)
        weights = jnp.where(mask, jnp.exp(scores - top), 0.0)
        total = jnp.sum(weights, axis=-1, keepdims=True)
        total = jnp.where(slot_len > 0.0, total, 1.0)
        probs = weights / total
        spread = jnp.concatenate(
            [jnp.where(of_slot == c, probs, 0.0) for c in range(cap)], axis=1
        ).astype(BF16)
        att[dev, k] = jnp.dot(spread, values, preferred_element_type=F32).astype(BF16)

    pl.semaphore_wait(barrier, NZ * NX)

    def att_copy(d, sem, where):
        return remote(att.at[d], att.at[d], att_send.at[sem], att_recv.at[d], where)

    att_out = [att_copy(dev, t - 1, to_z(t)) for t in range(1, NZ)]
    att_out.append(att_copy(dev, NZ - 1, to_x))
    for copy in att_out:
        copy.start()

    for i in range(EARLY, PAIRS - WO_PAIRS):
        start_pair(i)
    for b in range(WD_SLOTS):
        wd_copy(b).start()

    pos = iota((rows, 1), 0)
    each = rows // (NZ * NX * NH)
    row_of = ((pos // each) % NZ) * (NX * NH * each) + ((pos // (each * NZ)) % NX) * (NH * each)
    row_of = row_of + (pos // (each * NZ * NX)) * each + pos % each
    row_pick = across == row_of
    a_pos = jnp.sum(jnp.where(row_pick, a_row, 0.0), axis=1, keepdims=True)
    rank_pos = jnp.sum(
        jnp.where(row_pick, jnp.broadcast_to(rank_row, (rows, rows)), 0.0), axis=1, keepdims=True
    )
    target = a_pos * (group * cap) + rank_pos
    lane = iota((rows, NZ * NX * group * cap), 1).astype(F32)
    for g in range(group):
        place[g * rows:(g + 1) * rows, :] = jnp.where(lane == target + g * cap, 1.0, 0.0).astype(BF16)
    resid_half = resid_ref[:, pl.ds(pl.multiple_of(h * half, half), half)]
    mixed[...] = jnp.dot(row_pick.astype(F32).astype(BF16), resid_half, preferred_element_type=F32)

    for t in range(1, NZ):
        d = z_at(t) * NX + x
        att_copy(d, 0, to_x).wait_recv()
        fwd = att_copy(d, NZ - 1 + t, to_x)
        fwd.start()
        att_out.append(fwd)
    for t in range(NZ):
        d = z_at(t) * NX + other_x
        att_copy(d, 0, to_x).wait_recv()
    for k in range(kv):
        blocks = att[:, k].reshape(NZ * NX * group * cap, HD)
        moved = jnp.dot(place[...], blocks, preferred_element_type=F32).astype(BF16)
        for g in range(group):
            at = (k * group + g) * HD
            lhs[:, at:at + HD] = moved[g * rows:(g + 1) * rows, :]
    for copy in att_out:
        copy.wait_send()

    def project(start):
        cols = pl.ds(pl.multiple_of(start * half, half), half)
        total = None
        for j in range(2):
            depth = WO_PAIRS * half
            term = jnp.dot(
                lhs[:, j * depth:(j + 1) * depth],
                gu[j, 0:WO_PAIRS, :, cols].reshape(depth, half),
                preferred_element_type=F32,
            )
            total = term if total is None else total + term
        return total

    for m in range(2 * WO_PAIRS):
        wo_copy(m).wait()
    expart[...] = project(other_h)
    exchange = remote(expart, exrecv, ex_send, ex_recv, to_h)
    exchange.start()
    mixed[...] = mixed[...] + project(h)
    for i in range(PAIRS - WO_PAIRS, PAIRS):
        start_pair(i)
    exchange.wait()
    mix = mixed[...] + exrecv[...]
    mixed[...] = mix
    gains = gain_ref[0:1, pl.ds(pl.multiple_of(own * half, half), half)]
    nrm[own] = (mix * gains).astype(BF16)

    def nrm_copy(s, sem, where):
        return remote(nrm.at[s], nrm.at[s], nrm_send.at[sem], nrm_recv.at[s], where)

    for t in range(1, NZ):
        nrm_copy(own, t - 1, to_z(t)).start()
    nrm_copy(own, NZ - 1, to_x).start()
    nrm_copy(own, NZ, to_h).start()

    squares = jnp.sum(mix * mix, axis=1, keepdims=True)
    eye = iota((rows, HD), 0) == iota((rows, HD), 1)
    squares_row = jnp.sum(jnp.where(eye, squares, 0.0), axis=0, keepdims=True)
    sq[0] = jnp.broadcast_to(squares_row, (8, HD))

    def sq_copy(t):
        src, where = (0, to_z(t)) if t < NZ else ((NZ, to_x) if t == NZ else (NZ + 2, to_h))
        dst = t if t < NZ else (NZ + 1 if t == NZ else NZ + 3)
        return remote(sq.at[src], sq.at[dst], sq_send.at[t - 1], sq_recv.at[t - 1], where)

    for t in range(1, NZ):
        sq_copy(t).start()

    def arrived(i):
        nrm_copy(slab_at(i), 0, to_h).wait_recv()

    def pass_on(i, sem, where):
        nrm_copy(slab_at(i), sem, where).start()

    loaded = PAIRS
    for run in RUNS:
        first, count = run[0], len(run)
        if first == 1:
            arrived(2)
            pass_on(2, NZ + 1, to_h)
            arrived(1)
        elif first == 3:
            for i in run:
                arrived(i)
                pass_on(i, NZ - 1 + i, to_x)
                pass_on(i, 2 * NZ - 2 + i, to_h)
        elif first == 7:
            for i in run[:-1]:
                arrived(i)
                pass_on(i, 2 * NZ - 3 + i, to_h)
            arrived(run[-1])
            for t in range(1, NZ):
                sq_copy(t).wait()
            sq[NZ] = sq[0] + sq[1] + sq[2] + sq[3]
            sq_copy(NZ).start()
        elif first > 0:
            for i in run:
                arrived(i)
        if first == 11:
            sq_copy(NZ).wait()
            sq[NZ + 2] = sq[NZ] + sq[NZ + 1]
            sq_copy(NZ + 1).start()
        for i in run:
            gu_copy(i, 0).wait()
            gu_copy(i, 1).wait()
        slot = (first + WO_PAIRS) % PAIRS
        block = jnp.concatenate([nrm[slab_at(i)] for i in run], axis=1)

        def multiply_pair(j, carry, first=first, count=count, slot=slot, block=block):
            weight = gu[j, slot:slot + count].reshape(count * half, gu.shape[3])
            term = jnp.dot(block, weight, preferred_element_type=F32)
            acc[j] = term if first == 0 else acc[j] + term
            return carry

        lax.fori_loop(0, 2, multiply_pair, 0)
        for i in range(loaded, min(loaded + count, slabs)):
            start_pair(i)
        loaded = min(loaded + count, slabs)

    sq_copy(NZ + 1).wait()
    total_row = jnp.broadcast_to((sq[NZ + 2] + sq[NZ + 3])[0:1], (rows, HD))
    total = jnp.sum(jnp.where(eye, total_row, 0.0), axis=1, keepdims=True)
    scale = lax.rsqrt(total / D + 1e-05)
    gate = acc[0] * scale
    up = acc[1] * scale
    hidden[...] = (gate / (1.0 + jnp.exp(-gate)) * up).astype(BF16)

    batches = prod.shape[0]
    per = slabs // batches
    span = prod.shape[2]
    seg = zf.shape[3]
    hrows = rows // NH

    def multiply(b):
        wd_copy(b).wait()
        prod[b] = jnp.dot(hidden[...], wd[b % WD_SLOTS], preferred_element_type=F32)
        if b + WD_SLOTS < batches:
            wd_copy(b + WD_SLOTS).start()

        @pl.when(own // per == b)
        def _():
            cols = pl.ds(pl.multiple_of(lax.rem(own, per) * half, half), half)
            prod[b, :, cols] += mixed[...]

    def h_copy(b):
        src = prod.at[b, pl.ds(pl.multiple_of(other_h * hrows, hrows), hrows), :]
        return remote(src, hrecv.at[b], h_send.at[b], h_recv.at[b], to_h)

    def z_copy(b, p):
        zi, xi = chip(p)
        sem = b * (NZ * NX - 1) + p - 1
        src = zsend.at[b, xi * NZ + zi]
        return remote(src, zrecv.at[b, p - 1], z_send.at[sem], z_recv.at[sem], {"ffn": zi, "side": xi})

    def stage_z(b):
        h_copy(b).wait()
        s1[b] = prod[b, pl.ds(pl.multiple_of(h * hrows, hrows), hrows), :] + hrecv[b]
        for q in range(NZ * NX):
            for m in range(span // seg):
                zf[b, q, m * each:(m + 1) * each, :] = s1[b, q * each:(q + 1) * each, m * seg:(m + 1) * seg]
        zsend[b] = zf[b].astype(BF16)
        for p in (7, 6, 5, 4, 3, 2, 1):
            z_copy(b, p).start()

    def stage_out(b):
        total = zf[b, x * NZ + z]
        for p in range(1, NZ * NX):
            z_copy(b, p).wait()
            total = total + zrecv[b, p - 1].astype(F32)
        facc[b] = total
        for m in range(span // seg):
            at = b * span + m * seg
            out_ref[:, at:at + seg] = facc[b, m * each:(m + 1) * each, :].astype(BF16)

    for step in range(batches + 1):
        if step < batches:
            multiply(step)
            h_copy(step).start()
        if step >= 1:
            stage_z(step - 1)
    for b in range(batches):
        stage_out(b)

    for t in range(1, NZ):
        nrm_copy(own, t - 1, to_z(t)).wait_send()
    nrm_copy(own, NZ - 1, to_x).wait_send()
    nrm_copy(own, NZ, to_h).wait_send()
    nrm_copy(own, NZ + 1, to_h).wait_send()
    for i in range(3, 6):
        nrm_copy(own, NZ - 1 + i, to_x).wait_send()
        nrm_copy(own, 2 * NZ - 2 + i, to_h).wait_send()
    for i in range(7, 10):
        nrm_copy(own, 2 * NZ - 3 + i, to_h).wait_send()


def fused(
    resid, queries, cache_keys, cache_values, assign, lengths,
    out_weight, norm_gain, w_gate, w_up, w_down,
):
    rows, cols = resid.shape
    cap = queries.shape[0]
    ff = w_gate.shape[1]
    half = cols // NH
    slabs = NZ * NX * NH
    kv = cache_keys.shape[2] // HD
    group = queries.shape[1] // HD // kv
    batches = 4
    span = slabs * half // batches
    each = rows // slabs
    seg = span * each // 16
    vmem = pl.BlockSpec(memory_space=pltpu.VMEM)
    hbm = pl.BlockSpec(memory_space=pl.ANY)
    dma = pltpu.SemaphoreType.DMA
    V = pltpu.VMEM
    weights = (out_weight.size + 3 * w_gate.size)
    return pl.pallas_call(
        fused_kernel,
        out_shape=jax.ShapeDtypeStruct((each, slabs * half), BF16),
        in_specs=[vmem] * 7 + [hbm] * 4,
        out_specs=vmem,
        scratch_shapes=[
            V((2, PAIRS, half, ff), BF16),
            V((WD_SLOTS, ff, span), BF16),
            V((group * cap, HD), F32),
            V((group * rows, NZ * NX * group * cap), BF16),
            V((NZ * NX, kv, group * cap, HD), BF16),
            V((rows, out_weight.shape[0]), BF16),
            V((rows, half), F32),
            V((rows, half), F32),
            V((rows, half), F32),
            V((slabs, rows, half), BF16),
            V((NZ + 4, 8, HD), F32),
            V((2, rows, ff), F32),
            V((rows, ff), BF16),
            V((batches, rows, span), F32),
            V((batches, rows // NH, span), F32),
            V((batches, rows // NH, span), F32),
            V((batches, NZ * NX, 16, seg), F32),
            V((batches, NZ * NX, 16, seg), BF16),
            V((batches, NZ * NX - 1, 16, seg), BF16),
            V((batches, 16, seg), F32),
            dma((2 * WO_PAIRS,)),
            dma((2, PAIRS)),
            dma((WD_SLOTS,)),
            dma((2 * NZ,)),
            dma((NZ * NX,)),
            dma(()),
            dma(()),
            dma((4 * NZ - 1,)),
            dma((slabs,)),
            dma((NZ + 1,)),
            dma((NZ + 1,)),
            dma((batches,)),
            dma((batches,)),
            dma((batches * (NZ * NX - 1),)),
            dma((batches * (NZ * NX - 1),)),
        ],
        cost_estimate=pl.CostEstimate(
            flops=2 * rows * weights, bytes_accessed=2 * weights, transcendentals=rows * ff
        ),
        compiler_params=pltpu.CompilerParams(
            collective_id=0, has_side_effects=True, vmem_limit_bytes=63 * 1024 * 1024
        ),
    )(
        assign.reshape(1, rows), lengths.reshape(1, rows), norm_gain.reshape(1, -1),
        resid, queries, cache_keys, cache_values, out_weight, w_gate, w_up, w_down,
    )


def solution(mesh):
    in_specs = (
        P("groups", ("ffn", "side")),
        P(("groups", "ffn", "side"), "head"),
        P(("groups", "ffn", "side"), None, "head"),
        P(("groups", "ffn", "side"), None, "head"),
        P("groups"),
        P("groups"),
        P("head", ("ffn", "side")),
        P(),
        P(None, ("ffn", "side", "head")),
        P(None, ("ffn", "side", "head")),
        P(("ffn", "side", "head"), None),
    )
    out_specs = P(("groups", "ffn", "side", "head"), None)
    sizes = (mesh.shape["ffn"], mesh.shape["side"], mesh.shape["head"])
    body = fused if sizes == (NZ, NX, NH) else shards
    return jax.shard_map(body, mesh=mesh, in_specs=in_specs, out_specs=out_specs, check_vma=False)
```

```python
import functools

import jax
import jax.numpy as jnp
from jax import lax
from jax.experimental import pallas as pl
from jax.experimental.pallas import tpu as pltpu
from jax.sharding import PartitionSpec as P

D = 8192
HD = 128


def slot_numbers(assign, att_count, cap):
    owners = jnp.arange(att_count, dtype=jnp.int32)
    onehot = (assign[:, None] == owners[None, :]).astype(jnp.int32)
    before = jnp.cumsum(onehot, axis=0) - onehot
    rank = jnp.sum(before * onehot, axis=1)
    return assign * cap + rank


def shards(
    resid,
    queries,
    cache_keys,
    cache_values,
    assign,
    lengths,
    out_weight,
    norm_gain,
    w_gate,
    w_up,
    w_down,
):
    cap = queries.shape[0]
    ctx = cache_keys.shape[1]
    kv_local = cache_keys.shape[2] // HD
    q_local = queries.shape[1] // HD
    group = q_local // kv_local
    cols = resid.shape[1]
    att_count = lax.axis_size(("ffn", "side"))
    device = lax.axis_index(("ffn", "side"))
    slot_of = slot_numbers(assign, att_count, cap)
    wanted = device * cap + jnp.arange(cap, dtype=jnp.int32)
    match = slot_of[:, None] == wanted[None, :]
    slot_len = jnp.sum(jnp.where(match, lengths[:, None], 0), axis=0)
    qh = queries.reshape(cap, kv_local, group, HD)
    kh = cache_keys.reshape(cap, ctx, kv_local, HD)
    vh = cache_values.reshape(cap, ctx, kv_local, HD)
    scores = jnp.einsum("ckgd,ctkd->ckgt", qh, kh, preferred_element_type=jnp.float32) * (
        1.0 / float(HD) ** 0.5
    )
    mask = (jnp.arange(ctx, dtype=jnp.int32)[None, :] < slot_len[:, None])[:, None, None, :]
    top = jnp.max(jnp.where(mask, scores, -1e30), axis=-1, keepdims=True)
    weights = jnp.where(mask, jnp.exp(scores - top), 0.0)
    total = jnp.sum(weights, axis=-1, keepdims=True)
    total = jnp.where(slot_len[:, None, None, None] > 0, total, 1.0)
    probs = (weights / total).astype(jnp.bfloat16)
    attended = jnp.einsum("ckgt,ctkd->ckgd", probs, vh, preferred_element_type=jnp.float32)
    attended = attended.astype(jnp.bfloat16).reshape(cap, q_local * HD)
    partial_out = jnp.dot(
        lax.all_gather(attended, ("ffn", "side"), axis=0, tiled=True),
        out_weight,
        preferred_element_type=jnp.float32,
    )
    slot_out = lax.psum(partial_out, "head")
    mixed = resid.astype(jnp.float32) + jnp.take(slot_out, slot_of, axis=0)
    col_start = device * cols
    squares = jnp.sum(mixed * mixed, axis=1)
    meansq = lax.psum(squares, ("ffn", "side")) / D
    gain_local = lax.dynamic_slice_in_dim(norm_gain, col_start, cols, 0)
    normed = (mixed * lax.rsqrt(meansq + 1e-05)[:, None] * gain_local[None, :]).astype(jnp.bfloat16)
    piece = lax.all_gather(normed, ("ffn", "side"), axis=1, tiled=True)
    gate = jnp.dot(piece, w_gate, preferred_element_type=jnp.float32)
    up = jnp.dot(piece, w_up, preferred_element_type=jnp.float32)
    hidden = (jax.nn.silu(gate) * up).astype(jnp.bfloat16)
    product = jnp.dot(hidden, w_down, preferred_element_type=jnp.float32)
    carried = mixed * 0.5
    block = lax.dynamic_slice_in_dim(product, col_start, cols, 1) + carried
    summed = lax.psum_scatter(
        lax.dynamic_update_slice_in_dim(product, block, col_start, 1),
        ("ffn", "side", "head"),
        scatter_dimension=0,
        tiled=True,
    )
    return summed.astype(jnp.bfloat16)


NZ, NX, NH = 4, 2, 2
PAIRS = 11
WD_SLOTS = 3
WO_PAIRS = 4
EARLY = 2
RUNS = ((0,), (1,), (2,), (3, 4, 5, 6), (7, 8, 9), (10, 11, 12), (13, 14, 15))
STEPS = (
    (0, 0, 0), (0, 0, 1), (0, 1, 0), (0, 1, 1), (1, 0, 0), (2, 0, 0), (3, 0, 0), (1, 0, 1),
    (2, 0, 1), (3, 0, 1), (1, 1, 0), (2, 1, 0), (3, 1, 0), (1, 1, 1), (2, 1, 1), (3, 1, 1),
)
F32 = jnp.float32
BF16 = jnp.bfloat16


def iota(shape, dim):
    return lax.broadcasted_iota(jnp.int32, shape, dim)


def fused_kernel(
    assign_ref, lengths_ref, gain_ref, resid_ref, q_ref, k_ref, v_ref,
    wo_hbm, wg_hbm, wu_hbm, wd_hbm,
    out_ref,
    gu, wd, qf, place, att, lhs, expart, exrecv, mixed, nrm, sq, acc, hidden,
    prod, hrecv, s1, zf, zsend, zrecv, facc,
    wo_sem, gu_sem, wd_sem, att_send, att_recv, ex_send, ex_recv, nrm_send, nrm_recv,
    sq_send, sq_recv, h_send, h_recv, z_send, z_recv,
):
    z, x, h = lax.axis_index("ffn"), lax.axis_index("side"), lax.axis_index("head")
    dev = z * NX + x
    own = dev * NH + h
    other_x, other_h = 1 - x, 1 - h
    rows, width = lhs.shape
    half = nrm.shape[2]
    slabs = nrm.shape[0]
    cap = q_ref.shape[0]
    group = qf.shape[0] // cap
    kv = k_ref.shape[2] // HD

    def z_at(step):
        high = lax.rem(lax.div(z, 2) + step // 2, 2)
        return high * 2 + lax.rem(z + step, 2)

    def to_z(step):
        return {"ffn": z_at(step)}

    to_x, to_h = {"side": other_x}, {"head": other_h}

    def remote(src, dst, send, recv, where):
        return pltpu.make_async_remote_copy(
            src_ref=src, dst_ref=dst, send_sem=send, recv_sem=recv,
            device_id=where, device_id_type=pl.DeviceIdType.MESH,
        )

    def chip(p):
        return z_at(p // 2), lax.rem(x + p, NX)

    def slab_at(i):
        dz, dx, dh = STEPS[i]
        return (z_at(dz) * NX + lax.rem(x + dx, NX)) * NH + lax.rem(h + dh, NH)

    def wo_copy(m):
        src = wo_hbm.at[pl.ds(m * half, half), :]
        dst = gu.at[m // WO_PAIRS, m % WO_PAIRS, :, pl.ds(0, wo_hbm.shape[1])]
        return pltpu.make_async_copy(src, dst, wo_sem.at[m])

    def gu_copy(i, j):
        slot = (i + WO_PAIRS) % PAIRS
        src = (wg_hbm, wu_hbm)[j]
        start = pl.multiple_of(slab_at(i) * half, half)
        return pltpu.make_async_copy(src.at[pl.ds(start, half), :], gu.at[j, slot], gu_sem.at[j, slot])

    def wd_copy(b):
        slot = b % WD_SLOTS
        span = wd.shape[2]
        return pltpu.make_async_copy(wd_hbm.at[:, pl.ds(b * span, span)], wd.at[slot], wd_sem.at[slot])

    def start_pair(i):
        gu_copy(i, 0).start()
        gu_copy(i, 1).start()

    barrier = pltpu.get_barrier_semaphore()
    for p in range(1, NZ * NX):
        zi, xi = chip(p)
        where = {"ffn": zi, "side": xi}
        pl.semaphore_signal(barrier, inc=1, device_id=where, device_id_type=pl.DeviceIdType.MESH)
    pl.semaphore_signal(barrier, inc=1, device_id=to_h, device_id_type=pl.DeviceIdType.MESH)
    for m in range(2 * WO_PAIRS):
        wo_copy(m).start()
    for i in range(EARLY):
        start_pair(i)

    a_row = jnp.broadcast_to(assign_ref[...].astype(F32), (rows, rows))
    len_row = lengths_ref[...].astype(F32)
    down, across = iota((rows, rows), 0), iota((rows, rows), 1)
    a_col = jnp.sum(jnp.where(down == across, a_row, 0.0), axis=1, keepdims=True)
    rank_row = jnp.sum(
        jnp.where((a_col == a_row) & (down < across), 1.0, 0.0), axis=0, keepdims=True
    )
    slot_row = assign_ref[...].astype(F32) * cap + rank_row
    cr = iota((group * cap, 1), 0)
    of_slot = cr - cap * ((cr * 205) >> 10)
    wanted = (dev * cap + of_slot).astype(F32)
    slot_len = jnp.sum(
        jnp.where(jnp.broadcast_to(slot_row, (group * cap, rows)) == wanted, len_row, 0.0),
        axis=1, keepdims=True,
    )
    ctx = k_ref.shape[1]
    mask = iota((group * cap, ctx), 1).astype(F32) < slot_len
    for k in range(kv):
        for g in range(group):
            at = (k * group + g) * HD
            qf[g * cap:(g + 1) * cap, :] = q_ref[:, at:at + HD].astype(F32)
        qk = qf[...].astype(BF16)
        keys = k_ref[:, :, k * HD:(k + 1) * HD].reshape(cap * ctx, HD)
        values = v_ref[:, :, k * HD:(k + 1) * HD].reshape(cap * ctx, HD)
        wide = lax.dot_general(qk, keys, (((1,), (1,)), ((), ())), preferred_element_type=F32)
        scores = jnp.zeros((group * cap, ctx), F32)
        for c in range(cap):
            scores = jnp.where(of_slot == c, wide[:, c * ctx:(c + 1) * ctx], scores)
        scores = scores * (1.0 / float(HD) ** 0.5)
        top = jnp.max(jnp.where(mask, scores, -1e30), axis=-1, keepdims=True)
        weights = jnp.where(mask, jnp.exp(scores - top), 0.0)
        total = jnp.sum(weights, axis=-1, keepdims=True)
        total = jnp.where(slot_len > 0.0, total, 1.0)
        probs = weights / total
        spread = jnp.concatenate(
            [jnp.where(of_slot == c, probs, 0.0) for c in range(cap)], axis=1
        ).astype(BF16)
        att[dev, :, k * HD:(k + 1) * HD] = jnp.dot(
            spread, values, preferred_element_type=F32
        ).astype(BF16)

    pl.semaphore_wait(barrier, NZ * NX)

    def att_copy(d, sem, where, k):
        part = att.at[d, :, pl.ds(k * HD, HD)]
        return remote(part, part, att_send.at[k, sem], att_recv.at[k, d], where)

    att_out = []
    for k in range(kv):
        att_out.append(att_copy(dev, NZ - 1, to_x, k))
        att_out += [att_copy(dev, t - 1, to_z(t), k) for t in range(1, NZ)]
    for copy in att_out:
        copy.start()

    for i in range(EARLY, PAIRS - WO_PAIRS):
        start_pair(i)
    for b in range(WD_SLOTS):
        wd_copy(b).start()

    pos = iota((rows, 1), 0)
    each = rows // (NZ * NX * NH)
    row_of = ((pos // each) % NZ) * (NX * NH * each) + ((pos // (each * NZ)) % NX) * (NH * each)
    row_of = row_of + (pos // (each * NZ * NX)) * each + pos % each
    row_pick = across == row_of
    a_pos = jnp.sum(jnp.where(row_pick, a_row, 0.0), axis=1, keepdims=True)
    rank_pos = jnp.sum(
        jnp.where(row_pick, jnp.broadcast_to(rank_row, (rows, rows)), 0.0), axis=1, keepdims=True
    )
    target = a_pos * (group * cap) + rank_pos
    lane = iota((rows, NZ * NX * group * cap), 1).astype(F32)
    for g in range(group):
        place[g * rows:(g + 1) * rows, :] = jnp.where(lane == target + g * cap, 1.0, 0.0).astype(BF16)
    resid_half = resid_ref[:, pl.ds(pl.multiple_of(h * half, half), half)]
    mixed[...] = jnp.dot(row_pick.astype(F32).astype(BF16), resid_half, preferred_element_type=F32)

    for k in range(kv):
        for t in range(1, NZ):
            d = z_at(t) * NX + x
            att_copy(d, 0, to_x, k).wait_recv()
            fwd = att_copy(d, NZ - 1 + t, to_x, k)
            fwd.start()
            att_out.append(fwd)
    for k in range(kv):
        for t in range(NZ):
            d = z_at(t) * NX + other_x
            att_copy(d, 0, to_x, k).wait_recv()
    blocks = att[...].reshape(NZ * NX * group * cap, kv * HD)
    moved = jnp.dot(place[...], blocks, preferred_element_type=F32).astype(BF16)
    for k in range(kv):
        for g in range(group):
            at = (k * group + g) * HD
            lhs[:, at:at + HD] = moved[g * rows:(g + 1) * rows, k * HD:(k + 1) * HD]
    for copy in att_out:
        copy.wait_send()

    def project(start):
        cols = pl.ds(pl.multiple_of(start * half, half), half)
        total = None
        for j in range(2):
            depth = WO_PAIRS * half
            term = jnp.dot(
                lhs[:, j * depth:(j + 1) * depth],
                gu[j, 0:WO_PAIRS, :, cols].reshape(depth, half),
                preferred_element_type=F32,
            )
            total = term if total is None else total + term
        return total

    for m in range(2 * WO_PAIRS):
        wo_copy(m).wait()
    expart[...] = project(other_h)
    exchange = remote(expart, exrecv, ex_send, ex_recv, to_h)
    exchange.start()
    mixed[...] = mixed[...] + project(h)
    for i in range(PAIRS - WO_PAIRS, PAIRS):
        start_pair(i)
    exchange.wait()
    mix = mixed[...] + exrecv[...]
    mixed[...] = mix
    gains = gain_ref[0:1, pl.ds(pl.multiple_of(own * half, half), half)]
    nrm[own] = (mix * gains).astype(BF16)

    def nrm_copy(s, sem, where):
        return remote(nrm.at[s], nrm.at[s], nrm_send.at[sem], nrm_recv.at[s], where)

    nrm_copy(own, NZ, to_h).start()
    nrm_copy(own, NZ - 1, to_x).start()
    for t in range(1, NZ):
        nrm_copy(own, t - 1, to_z(t)).start()

    squares = jnp.sum(mix * mix, axis=1, keepdims=True)
    eye = iota((rows, HD), 0) == iota((rows, HD), 1)
    squares_row = jnp.sum(jnp.where(eye, squares, 0.0), axis=0, keepdims=True)
    sq[0] = jnp.broadcast_to(squares_row, (8, HD))

    def sq_copy(t):
        src, where = (0, to_z(t)) if t < NZ else ((NZ, to_x) if t == NZ else (NZ + 2, to_h))
        dst = t if t < NZ else (NZ + 1 if t == NZ else NZ + 3)
        return remote(sq.at[src], sq.at[dst], sq_send.at[t - 1], sq_recv.at[t - 1], where)

    for t in range(1, NZ):
        sq_copy(t).start()

    def arrived(i):
        nrm_copy(slab_at(i), 0, to_h).wait_recv()

    def pass_on(i, sem, where):
        nrm_copy(slab_at(i), sem, where).start()

    loaded = PAIRS
    for run in RUNS:
        first, count = run[0], len(run)
        if first == 2:
            arrived(2)
            pass_on(2, NZ + 1, to_h)
        elif first == 3:
            for i in run[1:]:
                arrived(i)
                pass_on(i, NZ - 2 + i, to_x)
                pass_on(i, 2 * NZ - 3 + i, to_h)
            arrived(3)
        elif first == 10:
            for i in run:
                arrived(i)
                pass_on(i, NZ - 2 + i, to_h)
        elif first > 0:
            for i in run:
                arrived(i)
        if first == 7:
            for t in range(1, NZ):
                sq_copy(t).wait()
            sq[NZ] = sq[0] + sq[1] + sq[2] + sq[3]
            sq_copy(NZ).start()
        elif first == 13:
            sq_copy(NZ).wait()
            sq[NZ + 2] = sq[NZ] + sq[NZ + 1]
            sq_copy(NZ + 1).start()
        for i in run:
            gu_copy(i, 0).wait()
            gu_copy(i, 1).wait()
        slot = (first + WO_PAIRS) % PAIRS
        block = jnp.concatenate([nrm[slab_at(i)] for i in run], axis=1)

        def multiply_pair(j, carry, first=first, count=count, slot=slot, block=block):
            weight = gu[j, slot:slot + count].reshape(count * half, gu.shape[3])
            term = jnp.dot(block, weight, preferred_element_type=F32)
            acc[j] = term if first == 0 else acc[j] + term
            return carry

        lax.fori_loop(0, 2, multiply_pair, 0)
        for i in range(loaded, min(loaded + count, slabs)):
            start_pair(i)
        loaded = min(loaded + count, slabs)

    sq_copy(NZ + 1).wait()
    total_row = jnp.broadcast_to((sq[NZ + 2] + sq[NZ + 3])[0:1], (rows, HD))
    total = jnp.sum(jnp.where(eye, total_row, 0.0), axis=1, keepdims=True)
    scale = lax.rsqrt(total / D + 1e-05)
    gate = acc[0] * scale
    up = acc[1] * scale
    hidden[...] = (gate / (1.0 + jnp.exp(-gate)) * up).astype(BF16)

    batches = prod.shape[0]
    per = slabs // batches
    span = prod.shape[2]
    seg = zf.shape[3]
    hrows = rows // NH

    def multiply(b):
        wd_copy(b).wait()
        prod[b] = jnp.dot(hidden[...], wd[b % WD_SLOTS], preferred_element_type=F32)
        if b + WD_SLOTS < batches:
            wd_copy(b + WD_SLOTS).start()

        @pl.when(own // per == b)
        def _():
            cols = pl.ds(pl.multiple_of(lax.rem(own, per) * half, half), half)
            prod[b, :, cols] += mixed[...]

    def h_copy(b):
        src = prod.at[b, pl.ds(pl.multiple_of(other_h * hrows, hrows), hrows), :]
        return remote(src, hrecv.at[b], h_send.at[b], h_recv.at[b], to_h)

    def z_copy(b, p):
        zi, xi = chip(p)
        sem = b * (NZ * NX - 1) + p - 1
        src = zsend.at[b, xi * NZ + zi]
        return remote(src, zrecv.at[b, p - 1], z_send.at[sem], z_recv.at[sem], {"ffn": zi, "side": xi})

    def stage_z(b):
        h_copy(b).wait()
        s1[b] = prod[b, pl.ds(pl.multiple_of(h * hrows, hrows), hrows), :] + hrecv[b]
        for q in range(NZ * NX):
            for m in range(span // seg):
                zf[b, q, m * each:(m + 1) * each, :] = s1[b, q * each:(q + 1) * each, m * seg:(m + 1) * seg]
        zsend[b] = zf[b].astype(BF16)
        for p in (7, 6, 5, 4, 3, 2, 1):
            z_copy(b, p).start()

    def stage_out(b):
        total = zf[b, x * NZ + z]
        for p in range(1, NZ * NX):
            z_copy(b, p).wait()
            total = total + zrecv[b, p - 1].astype(F32)
        facc[b] = total
        for m in range(span // seg):
            at = b * span + m * seg
            out_ref[:, at:at + seg] = facc[b, m * each:(m + 1) * each, :].astype(BF16)

    for step in range(batches + 1):
        if step < batches:
            multiply(step)
            h_copy(step).start()
        if step >= 1:
            stage_z(step - 1)
    for b in range(batches):
        stage_out(b)

    for t in range(1, NZ):
        nrm_copy(own, t - 1, to_z(t)).wait_send()
    nrm_copy(own, NZ - 1, to_x).wait_send()
    nrm_copy(own, NZ, to_h).wait_send()
    nrm_copy(own, NZ + 1, to_h).wait_send()
    for i in range(4, 7):
        nrm_copy(own, NZ - 2 + i, to_x).wait_send()
        nrm_copy(own, 2 * NZ - 3 + i, to_h).wait_send()
    for i in range(10, 13):
        nrm_copy(own, NZ - 2 + i, to_h).wait_send()


def fused(
    resid, queries, cache_keys, cache_values, assign, lengths,
    out_weight, norm_gain, w_gate, w_up, w_down,
):
    rows, cols = resid.shape
    cap = queries.shape[0]
    ff = w_gate.shape[1]
    half = cols // NH
    slabs = NZ * NX * NH
    kv = cache_keys.shape[2] // HD
    group = queries.shape[1] // HD // kv
    batches = 4
    span = slabs * half // batches
    each = rows // slabs
    seg = span * each // 16
    vmem = pl.BlockSpec(memory_space=pltpu.VMEM)
    hbm = pl.BlockSpec(memory_space=pl.ANY)
    dma = pltpu.SemaphoreType.DMA
    V = pltpu.VMEM
    weights = (out_weight.size + 3 * w_gate.size)
    return pl.pallas_call(
        fused_kernel,
        out_shape=jax.ShapeDtypeStruct((each, slabs * half), BF16),
        in_specs=[vmem] * 7 + [hbm] * 4,
        out_specs=vmem,
        scratch_shapes=[
            V((2, PAIRS, half, ff), BF16),
            V((WD_SLOTS, ff, span), BF16),
            V((group * cap, HD), F32),
            V((group * rows, NZ * NX * group * cap), BF16),
            V((NZ * NX, group * cap, kv * HD), BF16),
            V((rows, out_weight.shape[0]), BF16),
            V((rows, half), F32),
            V((rows, half), F32),
            V((rows, half), F32),
            V((slabs, rows, half), BF16),
            V((NZ + 4, 8, HD), F32),
            V((2, rows, ff), F32),
            V((rows, ff), BF16),
            V((batches, rows, span), F32),
            V((batches, rows // NH, span), F32),
            V((batches, rows // NH, span), F32),
            V((batches, NZ * NX, 16, seg), F32),
            V((batches, NZ * NX, 16, seg), BF16),
            V((batches, NZ * NX - 1, 16, seg), BF16),
            V((batches, 16, seg), F32),
            dma((2 * WO_PAIRS,)),
            dma((2, PAIRS)),
            dma((WD_SLOTS,)),
            dma((kv, 2 * NZ)),
            dma((kv, NZ * NX)),
            dma(()),
            dma(()),
            dma((4 * NZ - 1,)),
            dma((slabs,)),
            dma((NZ + 1,)),
            dma((NZ + 1,)),
            dma((batches,)),
            dma((batches,)),
            dma((batches * (NZ * NX - 1),)),
            dma((batches * (NZ * NX - 1),)),
        ],
        cost_estimate=pl.CostEstimate(
            flops=2 * rows * weights, bytes_accessed=2 * weights, transcendentals=rows * ff
        ),
        compiler_params=pltpu.CompilerParams(
            collective_id=0, has_side_effects=True, vmem_limit_bytes=63 * 1024 * 1024
        ),
    )(
        assign.reshape(1, rows), lengths.reshape(1, rows), norm_gain.reshape(1, -1),
        resid, queries, cache_keys, cache_values, out_weight, w_gate, w_up, w_down,
    )


def solution(mesh):
    in_specs = (
        P("groups", ("ffn", "side")),
        P(("groups", "ffn", "side"), "head"),
        P(("groups", "ffn", "side"), None, "head"),
        P(("groups", "ffn", "side"), None, "head"),
        P("groups"),
        P("groups"),
        P("head", ("ffn", "side")),
        P(),
        P(None, ("ffn", "side", "head")),
        P(None, ("ffn", "side", "head")),
        P(("ffn", "side", "head"), None),
    )
    out_specs = P(("groups", "ffn", "side", "head"), None)
    sizes = (mesh.shape["ffn"], mesh.shape["side"], mesh.shape["head"])
    body = fused if sizes == (NZ, NX, NH) else shards
    return jax.shard_map(body, mesh=mesh, in_specs=in_specs, out_specs=out_specs, check_vma=False)
```
